32 devices in a mesh: groups: 2 (over x), fsdp: 16 (over z, y, core).
Axes of the slice: x: 2, y: 2, z: 4, core: 2. Of those that a mesh axis runs over, the one named last changes fastest.
Arguments:
- tokens: bfloat16 [8192, 8192], P(('groups', 'fsdp')), parts along dimension 0, may hold values from -6 to 6
- key_weight: bfloat16 [8192, 1024], P('fsdp'), may hold values from -0.0625 to 0.0625
- adapter_down: bfloat16 [16384, 256], P(('groups', 'fsdp')), parts along dimension 0, may hold values from -0.0625 to 0.0625
- adapter_up: bfloat16 [512, 1024], P(('groups', 'fsdp')), parts along dimension 0, may hold values from -0.75 to 0.75
- key_cotangent: bfloat16 [8192, 1024], P(('groups', 'fsdp')), parts along dimension 0, may hold values from -6 to 6
- block_job: int32 [64], P('groups'), parts along dimension 0, may hold values from 0 to 3
- block_live: int32 [64], P(('groups', 'fsdp')), parts along dimension 0, may hold values from 1 to 128, as said below
- job_rank: int32 [8], P('groups'), parts along dimension 0, may hold values from 16 to 64, as said below
Outputs:
- keys: bfloat16 [8192, 1024], P(('groups', 'fsdp')), parts along dimension 0
- input_grad: bfloat16 [8192, 8192], P(('groups', 'fsdp')), parts along dimension 0
- down_grad: float32 [16384, 256], P(('groups', 'fsdp')), parts along dimension 0
- up_grad: float32 [512, 1024], P(('groups', 'fsdp')), parts along dimension 0
The draws below stay inside these ranges and needn't reach their ends.
There are 2 independent parts, one for each index of `groups`. The reference program is written for one: setup_inputs(seed, part) draws one part's arguments, and reference() takes and returns one part's arrays. A program takes and returns all parts, laid end to end along the dimension named above; an argument that names none is the same for every part. Nothing has to cross between parts.
Inputs may be any that keep to these rules, and one draw needn't show every extreme that they name: `block_live`: one block is full in every draw. `job_rank`: each rank is 16, 32 or 64; some job has rank 64 and some job rank 16.
All inputs are finite; a program needn't handle non-finite values.
Results may differ from the reference program's by a relative error of at most 0.0029.
Values may be sent and summed in bfloat16 or wider, within the bound.
No kernel may reach another device: no remote copies, remote signals or barrier semaphores. Data moves between devices by JAX's collectives and lax.ppermute only.
A program may use at most 128 MiB of HBM per device.

```python
import jax
import jax.numpy as jnp
from jax import lax

D = 8192
KV = 1024
RANK = 64
JOBS = 4
BLOCK = 128
TOKENS = 4096
BLOCKS = 32


def draw_block_live(key, part):
    key = jax.random.fold_in(key, 11)
    drawn = jax.random.randint(key, (BLOCKS,), 1, 2 * BLOCK)
    live_count = jnp.minimum(drawn, BLOCK)
    return live_count.at[0].set(BLOCK).astype(jnp.int32)


def draw_job_rank(key, part):
    key = jax.random.fold_in(key, 23)
    pick_key, place_key = jax.random.split(key)
    choose = jax.random.randint(pick_key, (JOBS,), 0, 3)
    place = jax.random.randint(place_key, (), 0, JOBS)
    indices = jnp.arange(JOBS, dtype=jnp.int32)
    choose = jnp.where(indices == place, 2, choose)
    choose = jnp.where(indices == (place + 1) % JOBS, 0, choose)
    ranks = jnp.where(choose == 0, 16, jnp.where(choose == 1, 32, 64))
    return ranks.astype(jnp.int32)


def set_ends(values, stream_key, low, top_value):
    dims = values.shape
    index_at = [jax.random.randint(jax.random.fold_in(stream_key, axis), (), 0, dims[axis]) for axis in range(len(dims))]
    values = values.at[tuple(index_at)].set(low)
    longest = dims.index(max(dims))
    index_at[longest] = (index_at[longest] + 1) % dims[longest]
    return values.at[tuple(index_at)].set(top_value)


def level_of(rng, dims, pieces, smallest, high):
    gain = 1.0
    for axis_at, shards_of in pieces:
        draws = jax.random.uniform(jax.random.fold_in(jax.random.fold_in(rng, 6), axis_at), (shards_of,), jnp.float32, smallest / len(pieces), high / len(pieces))
        gain = gain * jnp.repeat(jnp.exp(draws), dims[axis_at] // shards_of).reshape((-1,) + (1,) * (len(dims) - 1 - axis_at))
    return gain


def gaussian(stream_key, extent, deviation, reach, pieces=(), kind=jnp.bfloat16):
    gain = level_of(stream_key, extent, pieces, -0.22, 0.18) if pieces else 1.0
    values = jax.random.normal(stream_key, extent, jnp.float32) * deviation * gain
    return jnp.minimum(jnp.maximum(values, -reach), reach).astype(kind)


def setup_inputs(seed: int = 0, part: int = 0) -> dict:
    arg_keys = jax.random.split(jax.random.key(seed), 9)
    part_keys = jax.random.split(jax.random.fold_in(arg_keys[8], part), 9)
    tokens = gaussian(part_keys[0], (TOKENS, D), 1.0, 6.0, ((0, 16),))
    key_weight = gaussian(arg_keys[1], (D, KV), D ** -0.5, 0.0625, ((0, 16),))
    adapter_down = gaussian(part_keys[2], (D, JOBS * RANK), D ** -0.5, 0.0625, ((0, 16),))
    adapter_up = gaussian(part_keys[3], (JOBS * RANK, KV), RANK ** -0.5, 0.75, ((0, 16),))
    key_cotangent = gaussian(part_keys[4], (TOKENS, KV), 1.0, 6.0, ((0, 16),))
    block_job = set_ends(jax.random.randint(part_keys[5], (BLOCKS,), 0, JOBS), jax.random.fold_in(part_keys[5], 1), 0, JOBS - 1).astype(jnp.int32)
    block_live = draw_block_live(jax.random.fold_in(jax.random.fold_in(arg_keys[8], part), 71), part)
    job_rank = draw_job_rank(jax.random.fold_in(jax.random.fold_in(arg_keys[8], part), 71), part)
    return {"tokens": tokens, "key_weight": key_weight, "adapter_down": adapter_down, "adapter_up": adapter_up, "key_cotangent": key_cotangent, "block_job": block_job, "block_live": block_live, "job_rank": job_rank}


def reference(tokens, key_weight, adapter_down, adapter_up, key_cotangent, block_job, block_live, job_rank):
    position = jnp.arange(TOKENS, dtype=jnp.int32)
    tok_job = jnp.repeat(block_job, BLOCK)
    tok_live = jnp.repeat(block_live, BLOCK)
    live = (position % BLOCK < tok_live).astype(jnp.float32)
    columns = jnp.arange(JOBS * RANK, dtype=jnp.int32)
    col_job = columns // RANK
    col_rank = jnp.repeat(job_rank, RANK)
    col_scale = jnp.where(columns % RANK < col_rank, 16.0 / col_rank.astype(jnp.float32), 0.0).astype(jnp.float32)
    colmask = (col_job[None, :] == tok_job[:, None]).astype(jnp.float32) * col_scale[None, :] * live[:, None]
    low = (jnp.dot(tokens, adapter_down, preferred_element_type=jnp.float32) * colmask).astype(jnp.bfloat16)
    keys_full = jnp.dot(tokens, key_weight, preferred_element_type=jnp.float32) + jnp.dot(low, adapter_up, preferred_element_type=jnp.float32)
    keys = (keys_full * live[:, None]).astype(jnp.bfloat16)
    grad_keys = (key_cotangent.astype(jnp.float32) * live[:, None]).astype(jnp.bfloat16)
    grad_low = (jnp.dot(grad_keys, adapter_up.T, preferred_element_type=jnp.float32) * colmask).astype(jnp.bfloat16)
    input_grad = (jnp.dot(grad_keys, key_weight.T, preferred_element_type=jnp.float32) + jnp.dot(grad_low, adapter_down.T, preferred_element_type=jnp.float32)).astype(jnp.bfloat16)
    onehot = (block_job[:, None] == jnp.arange(JOBS, dtype=jnp.int32)[None, :]).astype(jnp.float32)
    count = lax.optimization_barrier(jnp.sum(onehot * block_live[:, None].astype(jnp.float32), axis=0))
    norm = jnp.repeat(1.0 / jnp.sqrt(jnp.maximum(count, 1.0)), RANK)
    contract = (((0,), (0,)), ((), ()))
    down_grad = lax.dot_general(tokens, grad_low, contract, preferred_element_type=jnp.float32) * norm[None, :]
    up_grad = lax.dot_general(low, grad_keys, contract, preferred_element_type=jnp.float32) * norm[:, None]
    return (keys, input_grad, down_grad, up_grad)
```

```python
import functools

import jax
import jax.numpy as jnp
from jax import lax
from jax.experimental import pallas as pl
from jax.experimental.pallas import tpu as pltpu
from jax.sharding import PartitionSpec as P

RANK = 64
BLOCK = 128


NT = (((1,), (1,)), ((), ()))
TN = (((0,), (0,)), ((), ()))


def pick_kernel(where, src, out):
    out[...] = src[...]


def pick_columns(where, tokens, shard):
    count = tokens.shape[0]
    blocks = where.shape[0]
    return pl.pallas_call(
        pick_kernel,
        grid_spec=pltpu.PrefetchScalarGridSpec(
            num_scalar_prefetch=1,
            grid=(blocks,),
            in_specs=[pl.BlockSpec((count, shard), lambda i, w: (0, w[i]))],
            out_specs=pl.BlockSpec((count, shard), lambda i, w: (0, i)),
        ),
        out_shape=jax.ShapeDtypeStruct((count, blocks * shard), tokens.dtype),
        cost_estimate=pl.CostEstimate(
            flops=0, bytes_accessed=4 * count * blocks * shard, transcendentals=0
        ),
    )(where, tokens)


def part_kernel(where, mine, theirs, low_mine, low_theirs, *refs):
    total = lax.dot_general(mine[...], low_mine[...], TN, preferred_element_type=jnp.float32)
    total += lax.dot_general(theirs[...], low_theirs[...], TN, preferred_element_type=jnp.float32)
    if len(refs) == 2:
        total += refs[0][...].astype(jnp.float32)
    refs[-1][...] = total.astype(refs[-1].dtype)


def part_sums(where, first, tokens, pair_tokens, low_mine, low_theirs, shard, received=None):
    count = tokens.shape[0]
    blocks = where.shape[0]
    low_width = low_mine.shape[1]
    whole = pl.BlockSpec((count, low_width), lambda i, w: (0, 0))
    rows = pl.BlockSpec((shard, low_width), lambda i, w: (i, 0))
    operands = [tokens, pair_tokens, low_mine, low_theirs]
    specs = [
        pl.BlockSpec((count, shard), lambda i, w: (0, w[i])),
        pl.BlockSpec((count, shard), lambda i, w: (0, first + i)),
        whole,
        whole,
    ]
    if received is not None:
        operands.append(received)
        specs.append(rows)
    return pl.pallas_call(
        part_kernel,
        grid_spec=pltpu.PrefetchScalarGridSpec(
            num_scalar_prefetch=1, grid=(blocks,), in_specs=specs, out_specs=rows
        ),
        out_shape=jax.ShapeDtypeStruct(
            (blocks * shard, low_width), jnp.bfloat16 if received is None else jnp.float32
        ),
        cost_estimate=pl.CostEstimate(
            flops=4 * count * blocks * shard * low_width,
            bytes_accessed=4 * count * blocks * shard,
            transcendentals=0,
        ),
    )(where, *operands)


def chunk_kernel(first, last, shard, where, *refs):
    tok, gk, gl, down = refs[:4]
    pieces, rest = refs[4:12], list(refs[12:])
    acc = None if first else rest.pop(0)
    low, up, live = (rest.pop(0) for _ in range(3)) if last else (None, None, None)
    if not first:
        rest.pop(0)
    ig, out = rest[:2]
    total = rest[2] if last else out
    y, c, g = where[1], where[2], where[3]
    half = shard // 2
    for j, ref in enumerate(pieces):
        yy = y if j < 4 else 1 - y
        core = c if j % 4 < 2 else 1 - c
        part = g if j % 2 == 0 else 1 - g
        at = pl.ds(pl.multiple_of(2 * shard * yy + shard * core + half * part, half), half)
        block = lax.dot_general(gk[...], ref[...], NT, preferred_element_type=jnp.float32)
        block += lax.dot_general(gl[...], down[at, :], NT, preferred_element_type=jnp.float32)
        ig[:, at] = block.astype(ig.dtype)
        term = jnp.dot(tok[:, at], ref[...], preferred_element_type=jnp.float32)
        if j == 0 and first:
            total[...] = term
        elif j == 0:
            total[...] = acc[...] + term
        else:
            total[...] += term
    if last:
        done = total[...] + jnp.dot(low[...], up[...], preferred_element_type=jnp.float32)
        out[...] = (done * live[...]).astype(out.dtype)


def chunk(where, tokens, gk, gl, down, pieces, acc, ig, ending=()):
    count, width = tokens.shape
    features = gk.shape[1]
    shard = 2 * pieces[0].shape[0]
    depth = 4 * shard
    first, last = acc is None, bool(ending)

    def whole(a):
        return pl.BlockSpec(a.shape, lambda i, w: (0, 0))

    operands = [tokens, gk, gl, down, *pieces]
    specs = [
        pl.BlockSpec((count, depth), lambda i, w: (0, w[0])),
        whole(gk),
        whole(gl),
        pl.BlockSpec((depth, down.shape[1]), lambda i, w: (w[0], 0)),
        *[whole(p) for p in pieces],
    ]
    if not first:
        operands.append(acc)
        specs.append(whole(acc))
    operands += ending
    specs += [whole(e) for e in ending]
    alias = {}
    if not first:
        alias = {len(operands) + 1: 0}
        operands.append(ig)
        specs.append(pl.BlockSpec(memory_space=pl.ANY))
    return pl.pallas_call(
        functools.partial(chunk_kernel, first, last, shard),
        grid_spec=pltpu.PrefetchScalarGridSpec(
            num_scalar_prefetch=1,
            grid=(1,),
            in_specs=specs,
            out_specs=[
                pl.BlockSpec((count, depth), lambda i, w: (0, w[0])),
                pl.BlockSpec((count, features), lambda i, w: (0, 0)),
            ],
            scratch_shapes=[pltpu.VMEM((count, features), jnp.float32)] if last else [],
        ),
        out_shape=[
            jax.ShapeDtypeStruct((count, width), jnp.bfloat16),
            jax.ShapeDtypeStruct((count, features), jnp.bfloat16 if last else jnp.float32),
        ],
        input_output_aliases=alias,
        compiler_params=pltpu.CompilerParams(vmem_limit_bytes=32 * 1024 * 1024),
        cost_estimate=pl.CostEstimate(
            flops=2 * count * depth * (2 * features + down.shape[1]),
            bytes_accessed=2 * depth * features + 4 * count * (depth + features),
            transcendentals=0,
        ),
    )(where, *operands)


def plain_form(
    tokens, key_weight, adapter_down, adapter_up, key_cotangent, block_job, block_live, job_rank
):
    tok_count = tokens.shape[0]
    jobs_here = job_rank.shape[0]
    width_low = adapter_down.shape[1]
    blocks_here = block_live.shape[0]
    my_index = lax.axis_index("fsdp")
    local_job = lax.dynamic_slice_in_dim(block_job, my_index * blocks_here, blocks_here, 0)
    weight_full, down_full = (
        lax.all_gather(key_weight, "fsdp", axis=0, tiled=True),
        lax.all_gather(adapter_down, "fsdp", axis=0, tiled=True),
    )
    up_full = lax.all_gather(adapter_up, "fsdp", axis=0, tiled=True)
    onehot = (local_job[:, None] == jnp.arange(jobs_here, dtype=jnp.int32)[None, :]).astype(
        jnp.float32
    )
    local_count = jnp.sum(onehot * block_live[:, None].astype(jnp.float32), axis=0)
    count = lax.psum(local_count, "fsdp")
    position = jnp.arange(tok_count, dtype=jnp.int32)
    tok_job = jnp.repeat(local_job, BLOCK)
    tok_live = jnp.repeat(block_live, BLOCK)
    live = (position % BLOCK < tok_live).astype(jnp.float32)
    columns = jnp.arange(width_low, dtype=jnp.int32)
    col_job = columns // RANK
    col_rank = jnp.repeat(job_rank, RANK)
    col_scale = jnp.where(columns % RANK < col_rank, 16.0 / col_rank.astype(jnp.float32), 0.0)
    colmask = (
        (col_job[None, :] == tok_job[:, None]).astype(jnp.float32)
        * col_scale[None, :]
        * live[:, None]
    )
    low = (jnp.dot(tokens, down_full, preferred_element_type=jnp.float32) * colmask).astype(
        jnp.bfloat16
    )
    keys_full = jnp.dot(tokens, weight_full, preferred_element_type=jnp.float32) + jnp.dot(
        low, up_full, preferred_element_type=jnp.float32
    )
    keys = (keys_full * live[:, None]).astype(jnp.bfloat16)
    grad_keys = (key_cotangent.astype(jnp.float32) * live[:, None]).astype(jnp.bfloat16)
    grad_low = (jnp.dot(grad_keys, up_full.T, preferred_element_type=jnp.float32) * colmask).astype(
        jnp.bfloat16
    )
    input_grad = (
        jnp.dot(grad_keys, weight_full.T, preferred_element_type=jnp.float32)
        + jnp.dot(grad_low, down_full.T, preferred_element_type=jnp.float32)
    ).astype(jnp.bfloat16)
    norm = jnp.repeat(1.0 / jnp.sqrt(jnp.maximum(count, 1.0)), RANK)
    contract = (((0,), (0,)), ((), ()))
    compact = jnp.sum(
        grad_low.astype(jnp.float32).reshape(tok_count, jobs_here, RANK), axis=1
    ).astype(jnp.bfloat16)
    compact_all = lax.all_gather(compact, "fsdp", axis=0, tiled=True)
    features = lax.all_to_all(tokens, "fsdp", split_axis=1, concat_axis=0, tiled=True)
    every_job = jnp.repeat(block_job, BLOCK)
    pieces = []
    for job_index in range(jobs_here):
        selected = compact_all * (every_job == job_index).astype(jnp.bfloat16)[:, None]
        pieces.append(
            lax.dot_general(features, selected, contract, preferred_element_type=jnp.float32)
        )
    owned = jnp.concatenate(pieces, axis=1)
    down_grad = owned * norm[None, :]
    up_term = lax.dot_general(low, grad_keys, contract, preferred_element_type=jnp.float32)
    up_owned = lax.psum_scatter(up_term, "fsdp", scatter_dimension=0, tiled=True)
    up_rows_here = adapter_up.shape[0]
    norm_rows = lax.dynamic_slice_in_dim(norm, my_index * up_rows_here, up_rows_here, 0)
    up_grad = up_owned * norm_rows[:, None]
    return (keys, input_grad, down_grad, up_grad)


def per_device(
    n, tokens, key_weight, adapter_down, adapter_up, key_cotangent, block_job, block_live, job_rank
):
    if n % 4 or key_weight.shape[0] % 256 or lax.axis_size("groups") != 2:
        return plain_form(
            tokens,
            key_weight,
            adapter_down,
            adapter_up,
            key_cotangent,
            block_job,
            block_live,
            job_rank,
        )
    f32, bf16 = jnp.float32, jnp.bfloat16
    outer = n // 4
    count, width = tokens.shape
    features = key_weight.shape[1]
    shard = key_weight.shape[0]
    jobs = job_rank.shape[0]
    low_width = adapter_down.shape[1]
    here = block_live.shape[0]
    idx = lax.axis_index("fsdp")
    g = lax.axis_index("groups")
    z, y, c = idx // 4, (idx // 2) % 2, idx % 2

    def swap(v, mask):
        return lax.ppermute(v, "fsdp", [(s, s ^ mask) for s in range(n)])

    def across(v):
        return lax.ppermute(v, "groups", [(0, 1), (1, 0)])

    def rows_of(v, i, size):
        return lax.dynamic_slice_in_dim(v, i * size, size, 0)

    local_job = rows_of(block_job, idx, here)
    pair_job = rows_of(block_job, idx ^ 1, here)
    position = jnp.arange(count, dtype=jnp.int32)
    live = (position % BLOCK < jnp.repeat(block_live, BLOCK)).astype(f32)
    columns = jnp.arange(low_width, dtype=jnp.int32)
    col_job = columns // RANK
    col_rank = jnp.repeat(job_rank, RANK)
    col_scale = jnp.where(columns % RANK < col_rank, 16.0 / col_rank.astype(f32), 0.0)

    def column_mask(job):
        mine = col_job[None, :] == jnp.repeat(job, BLOCK)[:, None]
        return mine.astype(f32) * col_scale[None, :]

    colmask = column_mask(local_job) * live[:, None]
    grad_keys = (key_cotangent.astype(f32) * live[:, None]).astype(bf16)

    up_rows = adapter_up.shape[0]
    tail = jnp.pad(block_live.astype(bf16), (0, 128 - here))
    packed = jnp.concatenate(
        [adapter_up, jnp.broadcast_to(tail[None, :], (up_rows, 128))], axis=1
    )
    gathered = jnp.concatenate(
        [packed] + [swap(packed, 4 * k) for k in range(1, outer)], axis=0
    )
    gathered = jnp.concatenate([gathered, swap(gathered, 2)], axis=0)
    gathered = jnp.concatenate([gathered, swap(gathered, 1)], axis=0)
    at = jnp.arange(n * up_rows, dtype=jnp.int32)
    place = at // up_rows
    mask = 4 * (place % outer) + 2 * (place // outer % 2) + place // (2 * outer)
    source = (idx ^ mask) * up_rows + at % up_rows
    order = (at[:, None] == source[None, :]).astype(bf16)
    ordered = jnp.dot(order, gathered, preferred_element_type=f32).astype(bf16)
    up_full = ordered[:, :features]
    live_all = ordered.reshape(n, up_rows, features + 128)[:, 0, features : features + here]
    live_all = live_all.reshape(n * here).astype(f32)
    onehot = (block_job[:, None] == jnp.arange(jobs, dtype=jnp.int32)[None, :]).astype(f32)
    count_of = jnp.sum(onehot * live_all[:, None], axis=0)
    norm = jnp.repeat(1.0 / jnp.sqrt(jnp.maximum(count_of, 1.0)), RANK)

    down_full = lax.all_gather(adapter_down, "fsdp", axis=0, tiled=True)

    places = 4 * jnp.arange(outer, dtype=jnp.int32)
    far_at, near_at = places + 2 * (1 - y) + c, places + 2 * y + c
    pair_keys = swap(grad_keys, 1)
    pair_tokens = swap(
        pick_columns(jnp.concatenate([far_at, near_at]) + 1 - 2 * c, tokens, shard), 1
    )

    def grad_low_of(keys, mask):
        return (
            lax.dot_general(keys, up_full, NT, preferred_element_type=f32) * mask
        ).astype(bf16)

    grad_low = grad_low_of(grad_keys, colmask)
    pair_low = grad_low_of(pair_keys, column_mask(pair_job))
    far = part_sums(far_at, 0, tokens, pair_tokens, grad_low, pair_low, shard)
    near = part_sums(
        near_at, outer, tokens, pair_tokens, grad_low, pair_low, shard, swap(far, 2)
    )
    owned = rows_of(near, z, shard)
    for k in range(1, outer):
        owned = owned + swap(rows_of(near, z ^ k, shard).astype(bf16), 4 * k).astype(f32)
    down_grad = owned * norm[None, :]

    low = (jnp.dot(tokens, down_full, preferred_element_type=f32) * colmask).astype(bf16)
    up_term = lax.dot_general(low, grad_keys, TN, preferred_element_type=f32)
    up_term = up_term.reshape(outer, 2, 2, up_rows, features)
    up_sum = lax.dynamic_index_in_dim(up_term, c, 2, False) + swap(
        lax.dynamic_index_in_dim(up_term, 1 - c, 2, False), 1
    )
    up_sum = lax.dynamic_index_in_dim(up_sum, y, 1, False) + swap(
        lax.dynamic_index_in_dim(up_sum, 1 - y, 1, False), 2
    )
    up_owned = lax.dynamic_index_in_dim(up_sum, z, 0, False)
    for k in range(1, outer):
        up_owned = up_owned + swap(lax.dynamic_index_in_dim(up_sum, z ^ k, 0, False), 4 * k)
    up_grad = up_owned * rows_of(norm, idx, up_rows)[:, None]

    half = shard // 2
    mine, rest = rows_of(key_weight, g, half), rows_of(key_weight, 1 - g, half)
    acc = ig = None
    for k in range(outer):
        near_half = mine if k == 0 else swap(mine, 4 * k)
        far_half = swap(near_half, 2)
        near_rest = rest if k == 0 else across(near_half)
        pieces = [near_half, near_rest, swap(near_half, 1), swap(near_rest, 1)]
        far_rest = across(far_half)
        pieces += [far_half, far_rest, swap(far_half, 1), swap(far_rest, 1)]
        where = jnp.stack([z ^ k, y, c, g]).astype(jnp.int32)
        ending = [low, up_full, live[:, None]] if k == outer - 1 else []
        ig, acc = chunk(
            where, tokens, grad_keys, grad_low, down_full, pieces, acc, ig, ending
        )
    return (acc, ig, down_grad, up_grad)


def solution(mesh):
    placed = (
        P(("groups", "fsdp"), None),
        P("fsdp", None),
        P(("groups", "fsdp"), None),
        P(("groups", "fsdp"), None),
        P(("groups", "fsdp"), None),
        P("groups"),
        P(("groups", "fsdp")),
        P("groups"),
    )
    return jax.shard_map(
        functools.partial(per_device, mesh.shape["fsdp"]),
        mesh=mesh,
        in_specs=placed,
        out_specs=(P(("groups", "fsdp"), None),) * 4,
        check_vma=False,
    )
```

```python
import functools

import jax
import jax.numpy as jnp
import numpy as np
from jax import lax
from jax.experimental import pallas as pl
from jax.experimental.pallas import tpu as pltpu
from jax.sharding import PartitionSpec as P

RANK = 64
BLOCK = 128
VMEM_LIMIT = 60 * 1024 * 1024


NT = (((1,), (1,)), ((), ()))
TN = (((0,), (0,)), ((), ()))


def takes(us):
    return pl.CostEstimate(flops=int(us * 1.15e9), bytes_accessed=int(us * 1e6), transcendentals=0)


def pick_kernel(shard, where, *refs):
    out = refs[-1]
    for j, src in enumerate(refs[:-1]):
        out[:, j * shard : (j + 1) * shard] = src[...]


def pick_columns(where, tokens, shard):
    count = tokens.shape[0]
    blocks = where.shape[0]
    return pl.pallas_call(
        functools.partial(pick_kernel, shard),
        grid_spec=pltpu.PrefetchScalarGridSpec(
            num_scalar_prefetch=1,
            grid=(1,),
            in_specs=[
                pl.BlockSpec((count, shard), lambda i, w, j=j: (0, w[j])) for j in range(blocks)
            ],
            out_specs=pl.BlockSpec((count, blocks * shard), lambda i, w: (0, 0)),
        ),
        out_shape=jax.ShapeDtypeStruct((count, blocks * shard), tokens.dtype),
        compiler_params=pltpu.CompilerParams(vmem_limit_bytes=VMEM_LIMIT),
        cost_estimate=takes(4),
    )(where, *[tokens] * blocks)


def part_kernel(blocks, shard, where, *refs):
    tokens, (theirs, low_mine, low_theirs), rest = refs[:blocks], refs[blocks : blocks + 3], refs[blocks + 3 :]
    for k in range(blocks):
        at = slice(k * shard, (k + 1) * shard)
        total = lax.dot_general(low_mine[...], tokens[k][...], TN, preferred_element_type=jnp.float32)
        total += lax.dot_general(
            low_theirs[...], theirs[:, at], TN, preferred_element_type=jnp.float32
        )
        if len(rest) == 1:
            rest[0][:, at] = total.astype(jnp.bfloat16)
            continue
        received, own, held, sent = rest
        total += received[:, at].astype(jnp.float32)
        if k == 0:
            own[...] = total
        elif k == 2:
            held[...] = total
        else:
            sent[:, (k // 2) * shard : (k // 2 + 1) * shard] = total.astype(jnp.bfloat16)


def part_sums(where, side, tokens, pair_tokens, low_mine, low_theirs, shard, received=None):
    count = tokens.shape[0]
    blocks = where.shape[0]
    low_width = low_mine.shape[1]

    def whole(rows, columns, at=0):
        return pl.BlockSpec((rows, columns), lambda i, w: (0, at))

    operands = [tokens] * blocks + [pair_tokens, low_mine, low_theirs]
    specs = [pl.BlockSpec((count, shard), lambda i, w, k=k: (0, w[k])) for k in range(blocks)]
    specs += [whole(count, blocks * shard, side)] + [whole(count, low_width)] * 2
    if received is None:
        shapes = [(blocks * shard, jnp.bfloat16)]
    else:
        operands.append(received)
        specs.append(whole(low_width, blocks * shard))
        shapes = [(shard, jnp.float32), (shard, jnp.float32), (2 * shard, jnp.bfloat16)]
    return pl.pallas_call(
        functools.partial(part_kernel, blocks, shard),
        grid_spec=pltpu.PrefetchScalarGridSpec(
            num_scalar_prefetch=1,
            grid=(1,),
            in_specs=specs,
            out_specs=[whole(low_width, columns) for columns, _ in shapes],
        ),
        out_shape=[jax.ShapeDtypeStruct((low_width, columns), kind) for columns, kind in shapes],
        compiler_params=pltpu.CompilerParams(vmem_limit_bytes=VMEM_LIMIT),
        cost_estimate=takes(4),
    )(where, *operands)


def finish_kernel(own, first, second, norm, out):
    total = own[...] + first[...].astype(jnp.float32) + second[...].astype(jnp.float32)
    out[...] = (total * norm[...]).T


def finish_sums(own, first, second, norm):
    rows, columns = own.shape

    def whole(a):
        return pl.BlockSpec(a, lambda i: (0, 0))

    return pl.pallas_call(
        finish_kernel,
        grid=(1,),
        in_specs=[whole((rows, columns))] * 3 + [whole((rows, 1))],
        out_specs=whole((columns, rows)),
        out_shape=jax.ShapeDtypeStruct((columns, rows), jnp.float32),
        compiler_params=pltpu.CompilerParams(vmem_limit_bytes=VMEM_LIMIT),
    )(own, first, second, norm)


def low_kernel(many, where, *refs):
    tokens, (pair_tokens, down, low, pair_low) = refs[:many], refs[many:]
    shard = tokens[0].shape[1]
    for j in range(many):
        rows = down[pl.ds(pl.multiple_of(where[2 * many + j] * shard, shard), shard), :]
        at = pl.ds(pl.multiple_of(where[many + j] * shard, shard), shard)
        mine = jnp.dot(tokens[j][...], rows, preferred_element_type=jnp.float32)
        theirs = jnp.dot(pair_tokens[:, at], rows, preferred_element_type=jnp.float32)
        if j == 0:
            low[...], pair_low[...] = mine, theirs
        else:
            low[...] += mine
            pair_low[...] += theirs


def low_sums(own_at, pair_at, down_at, tokens, pair_tokens, down, shard):
    count, low_width = tokens.shape[0], down.shape[1]
    many = own_at.shape[0]

    def whole(a):
        return pl.BlockSpec(a.shape, lambda i, w: (0, 0))

    out = pl.BlockSpec((count, low_width), lambda i, w: (0, 0))
    return pl.pallas_call(
        functools.partial(low_kernel, many),
        grid_spec=pltpu.PrefetchScalarGridSpec(
            num_scalar_prefetch=1,
            grid=(1,),
            in_specs=[
                pl.BlockSpec((count, shard), lambda i, w, j=j: (0, w[j])) for j in range(many)
            ]
            + [whole(pair_tokens), whole(down)],
            out_specs=[out, out],
        ),
        out_shape=[jax.ShapeDtypeStruct((count, low_width), jnp.float32)] * 2,
        compiler_params=pltpu.CompilerParams(vmem_limit_bytes=VMEM_LIMIT),
        cost_estimate=takes(5),
    )(jnp.concatenate([own_at, pair_at, down_at]), *[tokens] * many, pair_tokens, down)


def shards_kernel(first, many, old, where, *refs):
    refs = list(refs)
    take = lambda n: [refs.pop(0) for _ in range(n)]
    tok_in, pair_in = take(2)
    sides, pieces, (down_in,) = take(4), take(2 * many), take(1)
    before = [] if first else take(2)
    came = take(1) if old else []
    if not first:
        take(1)
    ig_out, pair_ig, acc, pair_acc = take(4)
    rows, down, both, keys, low, ig, held, sems, out_sems = take(9)
    half, count = pieces[0].shape[0], acc.shape[0]
    shard = 2 * half
    g = where[3 * many + old]
    used = [0]

    def load(source, target):
        copy = pltpu.make_async_copy(source, target, sems.at[used[0]])
        used[0] += 1
        copy.start()
        return copy

    def columns(at):
        return pl.ds(pl.multiple_of(at * shard, shard), shard)

    start = [
        load(sides[0], keys.at[:count]),
        load(sides[1], keys.at[count:]),
        load(sides[2], low.at[:count]),
        load(sides[3], low.at[count:]),
    ]
    loads = []
    for r in range(many):
        loads.append(
            [
                load(piece, rows.at[r, pl.ds(pl.multiple_of(part * half, half), half), :])
                for piece, part in ((pieces[2 * r], g), (pieces[2 * r + 1], 1 - g))
            ]
            + [
                load(down_in.at[columns(where[2 * many + r]), :], down.at[r]),
                load(tok_in.at[:, columns(where[r])], both.at[r, :count]),
                load(pair_in.at[:, columns(where[many + r])], both.at[r, count:]),
            ]
        )
        if r == 0:
            sums = [load(a, to) for a, to in zip(before, (acc, pair_acc))]
    arrived = [load(a, held) for a in came]
    for copy in start:
        copy.wait()
    stores = []

    def store(source, at):
        stores.append(
            pltpu.make_async_copy(source, ig_out.at[:, columns(at)], out_sems.at[len(stores)])
        )
        stores[-1].start()

    for r in range(many):
        for copy in loads[r]:
            copy.wait()
        block = lax.dot_general(keys[...], rows[r], NT, preferred_element_type=jnp.float32)
        block += lax.dot_general(low[...], down[r], NT, preferred_element_type=jnp.float32)
        ig[r] = block[:count].astype(ig.dtype)
        pair_ig[:, r * shard : (r + 1) * shard] = block[count:].astype(ig.dtype)
        store(ig.at[r], where[r])
        term = jnp.dot(both[r], rows[r], preferred_element_type=jnp.float32)
        if r == 0:
            for copy in sums:
                copy.wait()
        if r == 0 and first:
            acc[...], pair_acc[...] = term[:count], term[count:]
        else:
            acc[...] += term[:count]
            pair_acc[...] += term[count:]
        if r == 0:
            for copy in arrived:
                copy.wait()
            for j in range(old):
                store(held.at[:, j * shard : (j + 1) * shard], where[3 * many + j])
    for copy in stores:
        copy.wait()


def add_shards(where, tokens, pair_tokens, sides, pieces, down, acc, came, ig):
    count, width = tokens.shape
    features = pieces[0].shape[1]
    many = len(pieces) // 2
    shard, low_width = 2 * pieces[0].shape[0], down.shape[1]
    first = acc is None
    old = 0 if came is None else came.shape[1] // shard
    operands = [tokens, pair_tokens, *sides, *pieces, down]
    if not first:
        operands += acc
    if old:
        operands.append(came)
    alias = {}
    if not first:
        alias = {len(operands) + 1: 0}
        operands.append(ig)
    bf16 = jnp.bfloat16
    sums = pl.BlockSpec((count, features), lambda i, w: (0, 0))
    ig, pair_ig, *acc = pl.pallas_call(
        functools.partial(shards_kernel, first, many, old),
        grid_spec=pltpu.PrefetchScalarGridSpec(
            num_scalar_prefetch=1,
            grid=(1,),
            in_specs=[pl.BlockSpec(memory_space=pl.ANY)] * len(operands),
            out_specs=[
                pl.BlockSpec(memory_space=pl.ANY),
                pl.BlockSpec((count, many * shard), lambda i, w: (0, 0)),
                sums,
                sums,
            ],
            scratch_shapes=[
                pltpu.VMEM((many, shard, features), bf16),
                pltpu.VMEM((many, shard, low_width), bf16),
                pltpu.VMEM((many, 2 * count, shard), bf16),
                pltpu.VMEM((2 * count, features), bf16),
                pltpu.VMEM((2 * count, low_width), bf16),
                pltpu.VMEM((many, count, shard), bf16),
                pltpu.VMEM((count, max(old, 1) * shard), bf16),
                pltpu.SemaphoreType.DMA((7 + 5 * many,)),
                pltpu.SemaphoreType.DMA((many + old,)),
            ],
        ),
        out_shape=[
            jax.ShapeDtypeStruct((count, width), bf16),
            jax.ShapeDtypeStruct((count, many * shard), bf16),
            jax.ShapeDtypeStruct((count, features), jnp.float32),
            jax.ShapeDtypeStruct((count, features), jnp.float32),
        ],
        input_output_aliases=alias,
        compiler_params=pltpu.CompilerParams(vmem_limit_bytes=VMEM_LIMIT),
        cost_estimate=takes(3 + 1.5 * many),
    )(where, *operands)
    return ig, pair_ig, acc


def insert_kernel(blocks, where, received, *refs):
    sems, out = refs[-1], refs[-2] if len(refs) == 3 else refs[-3]
    shard = received.shape[1] // blocks
    copies = []
    for j in range(blocks):
        to = pl.ds(pl.multiple_of(where[j] * shard, shard), shard)
        copies.append(
            pltpu.make_async_copy(
                received.at[:, j * shard : (j + 1) * shard], out.at[:, to], sems.at[j]
            )
        )
        copies[-1].start()
    if len(refs) > 3:
        low, up, acc, theirs, live, _, _, keys, _ = refs
        total = acc[...] + theirs[...]
        total += jnp.dot(low[...], up[...], preferred_element_type=jnp.float32)
        keys[...] = (total * live[...]).astype(keys.dtype)
    for copy in copies:
        copy.wait()


def insert(where, received, ig, ending=()):
    count, width = ig.shape
    blocks = where.shape[0]

    def whole(a):
        return pl.BlockSpec(a.shape, lambda i, w: (0, 0))

    outs = [pl.BlockSpec(memory_space=pl.ANY)]
    shapes = [jax.ShapeDtypeStruct(ig.shape, ig.dtype)]
    if ending:
        features = ending[2].shape[1]
        outs.append(pl.BlockSpec((count, features), lambda i, w: (0, 0)))
        shapes.append(jax.ShapeDtypeStruct((count, features), ig.dtype))
    return pl.pallas_call(
        functools.partial(insert_kernel, blocks),
        grid_spec=pltpu.PrefetchScalarGridSpec(
            num_scalar_prefetch=1,
            grid=(1,),
            in_specs=[whole(a) for a in (received, *ending)]
            + [pl.BlockSpec(memory_space=pl.ANY)],
            out_specs=outs,
            scratch_shapes=[pltpu.SemaphoreType.DMA((blocks,))],
        ),
        out_shape=shapes,
        input_output_aliases={2 + len(ending): 0},
        compiler_params=pltpu.CompilerParams(vmem_limit_bytes=VMEM_LIMIT),
        cost_estimate=takes(2.5),
    )(where, received, *ending, ig)


def plain_form(
    tokens, key_weight, adapter_down, adapter_up, key_cotangent, block_job, block_live, job_rank
):
    tok_count = tokens.shape[0]
    jobs_here = job_rank.shape[0]
    width_low = adapter_down.shape[1]
    blocks_here = block_live.shape[0]
    my_index = lax.axis_index("fsdp")
    local_job = lax.dynamic_slice_in_dim(block_job, my_index * blocks_here, blocks_here, 0)
    weight_full, down_full = (
        lax.all_gather(key_weight, "fsdp", axis=0, tiled=True),
        lax.all_gather(adapter_down, "fsdp", axis=0, tiled=True),
    )
    up_full = lax.all_gather(adapter_up, "fsdp", axis=0, tiled=True)
    onehot = (local_job[:, None] == jnp.arange(jobs_here, dtype=jnp.int32)[None, :]).astype(
        jnp.float32
    )
    local_count = jnp.sum(onehot * block_live[:, None].astype(jnp.float32), axis=0)
    count = lax.psum(local_count, "fsdp")
    position = jnp.arange(tok_count, dtype=jnp.int32)
    tok_job = jnp.repeat(local_job, BLOCK)
    tok_live = jnp.repeat(block_live, BLOCK)
    live = (position % BLOCK < tok_live).astype(jnp.float32)
    columns = jnp.arange(width_low, dtype=jnp.int32)
    col_job = columns // RANK
    col_rank = jnp.repeat(job_rank, RANK)
    col_scale = jnp.where(columns % RANK < col_rank, 16.0 / col_rank.astype(jnp.float32), 0.0)
    colmask = (
        (col_job[None, :] == tok_job[:, None]).astype(jnp.float32)
        * col_scale[None, :]
        * live[:, None]
    )
    low = (jnp.dot(tokens, down_full, preferred_element_type=jnp.float32) * colmask).astype(
        jnp.bfloat16
    )
    keys_full = jnp.dot(tokens, weight_full, preferred_element_type=jnp.float32) + jnp.dot(
        low, up_full, preferred_element_type=jnp.float32
    )
    keys = (keys_full * live[:, None]).astype(jnp.bfloat16)
    grad_keys = (key_cotangent.astype(jnp.float32) * live[:, None]).astype(jnp.bfloat16)
    grad_low = (jnp.dot(grad_keys, up_full.T, preferred_element_type=jnp.float32) * colmask).astype(
        jnp.bfloat16
    )
    input_grad = (
        jnp.dot(grad_keys, weight_full.T, preferred_element_type=jnp.float32)
        + jnp.dot(grad_low, down_full.T, preferred_element_type=jnp.float32)
    ).astype(jnp.bfloat16)
    norm = jnp.repeat(1.0 / jnp.sqrt(jnp.maximum(count, 1.0)), RANK)
    contract = (((0,), (0,)), ((), ()))
    compact = jnp.sum(
        grad_low.astype(jnp.float32).reshape(tok_count, jobs_here, RANK), axis=1
    ).astype(jnp.bfloat16)
    compact_all = lax.all_gather(compact, "fsdp", axis=0, tiled=True)
    features = lax.all_to_all(tokens, "fsdp", split_axis=1, concat_axis=0, tiled=True)
    every_job = jnp.repeat(block_job, BLOCK)
    pieces = []
    for job_index in range(jobs_here):
        selected = compact_all * (every_job == job_index).astype(jnp.bfloat16)[:, None]
        pieces.append(
            lax.dot_general(features, selected, contract, preferred_element_type=jnp.float32)
        )
    owned = jnp.concatenate(pieces, axis=1)
    down_grad = owned * norm[None, :]
    up_term = lax.dot_general(low, grad_keys, contract, preferred_element_type=jnp.float32)
    up_owned = lax.psum_scatter(up_term, "fsdp", scatter_dimension=0, tiled=True)
    up_rows_here = adapter_up.shape[0]
    norm_rows = lax.dynamic_slice_in_dim(norm, my_index * up_rows_here, up_rows_here, 0)
    up_grad = up_owned * norm_rows[:, None]
    return (keys, input_grad, down_grad, up_grad)


def per_device(
    n, tokens, key_weight, adapter_down, adapter_up, key_cotangent, block_job, block_live, job_rank
):
    if n != 16 or key_weight.shape[0] % 512 or lax.axis_size("groups") != 2:
        return plain_form(
            tokens,
            key_weight,
            adapter_down,
            adapter_up,
            key_cotangent,
            block_job,
            block_live,
            job_rank,
        )
    f32, bf16 = jnp.float32, jnp.bfloat16
    outer = n // 4
    count, width = tokens.shape
    features = key_weight.shape[1]
    shard = key_weight.shape[0]
    jobs = job_rank.shape[0]
    low_width = adapter_down.shape[1]
    here = block_live.shape[0]
    idx = lax.axis_index("fsdp")
    g = lax.axis_index("groups")
    z, y, c = idx // 4, (idx // 2) % 2, idx % 2

    def swap(v, mask):
        return lax.ppermute(v, "fsdp", [(s, s ^ mask) for s in range(n)])

    def across(v):
        return lax.ppermute(v, "groups", [(0, 1), (1, 0)])

    def rows_of(v, i, size):
        return lax.dynamic_slice_in_dim(v, i * size, size, 0)

    local_job = rows_of(block_job, idx, here)
    pair_job = rows_of(block_job, idx ^ 1, here)
    position = jnp.arange(count, dtype=jnp.int32)
    live = (position % BLOCK < jnp.repeat(block_live, BLOCK)).astype(f32)
    columns = jnp.arange(low_width, dtype=jnp.int32)
    col_job = columns // RANK
    col_rank = jnp.repeat(job_rank, RANK)
    col_scale = jnp.where(columns % RANK < col_rank, 16.0 / col_rank.astype(f32), 0.0)

    def column_mask(job):
        mine = col_job[None, :] == jnp.repeat(job, BLOCK)[:, None]
        return mine.astype(f32) * col_scale[None, :]

    colmask = column_mask(local_job) * live[:, None]
    grad_keys = (key_cotangent.astype(f32) * live[:, None]).astype(bf16)

    def after(done, *values):
        values = lax.optimization_barrier((tuple(values), tuple(done)))[0]
        return values if len(values) > 1 else values[0]

    half = shard // 2
    mine, rest = rows_of(key_weight, g, half), rows_of(key_weight, 1 - g, half)

    def after(done, *values):
        values = lax.optimization_barrier((tuple(values), tuple(done)))[0]
        return values if len(values) > 1 else values[0]

    last = {}

    def send(link, go, value, *also):
        if link in last or also:
            value = after(last.get(link, []) + list(also), value)
        got = go(value)
        last[link] = [got]
        return got

    def beside(value, *also):
        return send("y", lambda v: swap(v, 2), value, *also)

    def along(value, mask, *also):
        return send("z", lambda v: swap(v, mask), value, *also)

    def over(value, *also):
        return send("x", across, value, *also)

    half = shard // 2
    mine, rest = rows_of(key_weight, g, half), rows_of(key_weight, 1 - g, half)
    near, far = [mine, swap(mine, 4), swap(mine, 8)], [beside(mine)]
    last["z"] = near[1:]
    far_rest = [over(far[0])]
    near_rest = [rest, over(near[1])]

    up_rows = adapter_up.shape[0]
    tail = jnp.pad(block_live.astype(bf16), (0, 128 - here))
    packed = jnp.concatenate(
        [adapter_up, jnp.broadcast_to(tail[None, :], (up_rows, 128))], axis=1
    )
    gathered = jnp.concatenate([packed, swap(after(far, packed), 2)], axis=0)
    gathered = after(near[1:] + far_rest, gathered)
    gathered = jnp.concatenate([gathered, swap(gathered, 4)], axis=0)
    gathered = after(near_rest[1:], gathered)
    gathered = jnp.concatenate([gathered, swap(gathered, 8)], axis=0)
    gathered = jnp.concatenate([gathered, swap(gathered, 1)], axis=0)
    at = jnp.arange(n * up_rows, dtype=jnp.int32)
    place = at // up_rows
    mask = 2 * (place % 2) + 4 * (place // 2 % outer) + place // (2 * outer)
    source = (idx ^ mask) * up_rows + at % up_rows
    order = (at[:, None] == source[None, :]).astype(bf16)
    ordered = jnp.dot(order, gathered, preferred_element_type=f32).astype(bf16)

    same_core = [[q for q in range(n) if q % 2 == p] for p in range(2)]
    down_rows = lax.all_gather(
        adapter_down, "fsdp", axis=0, tiled=True, axis_index_groups=same_core
    )

    relative = jnp.arange(outer, dtype=jnp.int32)
    near_at = 4 * (z ^ relative) + 2 * y + c
    far_at = near_at + 2 - 4 * y
    pair_keys = swap(grad_keys, 1)
    pair_tokens = swap(
        pick_columns(jnp.concatenate([far_at, near_at]) + 1 - 2 * c, tokens, shard), 1
    )

    far.append(beside(near[1]))
    far_rest.append(over(far[1]))
    near_rest.append(over(near[2]))
    far.append(beside(near[2]))
    near.append(along(near[2], 4))
    near_rest.append(along(near_rest[2], 4))

    up_full = ordered[:, :features]
    live_all = ordered.reshape(n, up_rows, features + 128)[:, 0, features : features + here]
    live_all = live_all.reshape(n * here).astype(f32)
    onehot = (block_job[:, None] == jnp.arange(jobs, dtype=jnp.int32)[None, :]).astype(f32)
    count_of = jnp.sum(onehot * live_all[:, None], axis=0)
    norm = jnp.repeat(1.0 / jnp.sqrt(jnp.maximum(count_of, 1.0)), RANK)

    def grad_low_of(keys, mask):
        return (
            lax.dot_general(keys, up_full, NT, preferred_element_type=f32) * mask
        ).astype(bf16)

    grad_low = grad_low_of(grad_keys, colmask)
    pair_low = grad_low_of(pair_keys, column_mask(pair_job))
    (part_far,) = part_sums(far_at, 0, tokens, pair_tokens, grad_low, pair_low, shard)
    part_swapped = beside(part_far)
    far.append(beside(near[3]))
    far_rest.append(over(far[2]))
    far_rest.append(over(far[3]))

    own, held, sent = part_sums(
        near_at, 1, tokens, pair_tokens, grad_low, pair_low, shard, part_swapped
    )
    first = along(sent, 4)
    second = along((held + first[:, shard:].astype(f32)).astype(bf16), 8)

    sides = [grad_keys, pair_keys, grad_low, pair_low]
    order_of = [(k, d) for k in range(outer) for d in range(2)]

    def places(shards):
        k = np.array([s[0] for s in shards], np.int32)
        d = np.array([s[1] for s in shards], np.int32)
        own = 4 * (z ^ k) + 2 * (y ^ d) + c
        return own, outer - outer * d + k, 2 * (z ^ k) + (y ^ d)

    def run(shards, acc, came, ig):
        pieces = []
        for k, distant in shards:
            pieces += [far[k], far_rest[k]] if distant else [near[k], near_rest[k]]
        own, pair, row = places(shards)
        at, came = ([], None) if came is None else ([came[0]], came[1])
        where = jnp.concatenate([own, pair, row] + at + [jnp.broadcast_to(g, (1,))])
        ig, pair_ig, acc = add_shards(
            where.astype(jnp.int32), tokens, pair_tokens, sides, pieces, down_rows, acc, came, ig
        )
        return ig, (own + 1 - 2 * c, swap(pair_ig, 1)), acc

    sides[2] = after([sent], sides[2])
    ig, came, acc = run(((0, 0), (0, 1), (1, 0), (1, 1)), None, None, None)
    low, pair_sum = low_sums(
        *places(order_of),
        tokens,
        pair_tokens,
        down_rows,
        shard,
    )
    low = ((low + swap(pair_sum, 1)) * colmask).astype(bf16)
    up_term = lax.dot_general(low, grad_keys, TN, preferred_element_type=f32)
    up_term = up_term.reshape(outer, 2, 2, up_rows, features)
    up_sum = lax.dynamic_index_in_dim(up_term, c, 2, False) + swap(
        lax.dynamic_index_in_dim(up_term, 1 - c, 2, False), 1
    )
    up_sum = lax.dynamic_index_in_dim(up_sum, y, 1, False) + swap(
        lax.dynamic_index_in_dim(up_sum, 1 - y, 1, False), 2
    )
    up_owned = lax.dynamic_index_in_dim(up_sum, z, 0, False)
    acc[0] = after([first, up_sum], acc[0])
    ig, came, acc = run(((2, 0), (2, 1)), acc, came, ig)
    for k in range(1, outer):
        sent_up = lax.dynamic_index_in_dim(up_sum, z ^ k, 0, False)
        up_owned = up_owned + swap(sent_up, 4 * k)
    up_grad = up_owned * rows_of(norm, idx, up_rows)[:, None]
    down_grad = finish_sums(own, first, second, norm[:, None])

    acc[0] = after([down_grad, up_grad], acc[0])
    ig, came, acc = run(((3, 0), (3, 1)), acc, came, ig)
    ending = [low, up_full, acc[0], swap(acc[1], 1), live[:, None]]
    ig, keys = insert(*came, ig, ending)
    return (keys, ig, down_grad, up_grad)


def solution(mesh):
    placed = (
        P(("groups", "fsdp"), None),
        P("fsdp", None),
        P(("groups", "fsdp"), None),
        P(("groups", "fsdp"), None),
        P(("groups", "fsdp"), None),
        P("groups"),
        P(("groups", "fsdp")),
        P("groups"),
    )
    return jax.shard_map(
        functools.partial(per_device, mesh.shape["fsdp"]),
        mesh=mesh,
        in_specs=placed,
        out_specs=(P(("groups", "fsdp"), None),) * 4,
        check_vma=False,
    )
```
